32 devices in a mesh: hid: 4 (over y, x), wid: 8 (over z, core).
Axes of the slice: x: 2, y: 2, z: 4, core: 2. Of those that a mesh axis runs over, the one named last changes fastest.
Arguments:
- tokens: bfloat16 [512, 16384], P(None, 'wid'), may hold values from -6 to 6
- gate_quant: bfloat16 [16384, 26624], P('wid', 'hid'), may hold values from -0.046875 to 0.046875
- gate_scale: float32 [128, 208], P('wid', 'hid'), may hold values from 0.25 to 4
- up_quant: bfloat16 [16384, 26624], P('wid', 'hid'), may hold values from -0.046875 to 0.046875
- up_scale: float32 [128, 208], P('wid', 'hid'), may hold values from 0.25 to 4
- down_quant: bfloat16 [26624, 16384], P('hid', 'wid'), may hold values from -0.0390625 to 0.0390625
- down_scale: float32 [208, 128], P('hid', 'wid'), may hold values from 0.25 to 4
Outputs:
- mixed: bfloat16 [512, 16384], P(None, 'wid')
The draws below stay inside these ranges and needn't reach their ends.
All inputs are finite; a program needn't handle non-finite values.
Results may differ from the reference program's by a relative error of at most 0.03.
Values may be sent and summed in bfloat16 or wider, within the bound.
A program may use at most 256 MiB of HBM per device.

```python
import math
import jax
import jax.numpy as jnp
from jax import lax

D = 16384
FFW = 26624
BLK = 128
ROWS = 512
N_WID = 8


def block_scale(stream_key, shape, shards, smallest, largest):
    def one(dim, shards_of):
        heights = jax.random.uniform(jax.random.fold_in(jax.random.fold_in(stream_key, 6), dim), (shards_of,), jnp.float32, smallest / len(shards), largest / len(shards))
        return jnp.repeat(jnp.exp(heights), shape[dim] // shards_of).reshape((-1,) + (1,) * (len(shape) - dim - 1))

    loudness = one(*shards[0])
    for cut in shards[1:]:
        loudness = loudness * one(*cut)
    return loudness


def normal_values(rng, shape, spread, limit, split=(), held_as=jnp.bfloat16):
    result = spread * jax.random.normal(rng, shape, jnp.float32)
    if split:
        result = result * block_scale(rng, shape, split, -0.22, 0.18)
    return jnp.clip(result, -limit, limit).astype(held_as)


def setup_inputs(seed: int = 0) -> dict:
    seeds = jax.random.split(jax.random.key(seed), 8)
    tokens = normal_values(seeds[0], (ROWS, D), 1.0, 6.0, ((1, 8),))
    gate_quant = normal_values(seeds[1], (D, FFW), D ** -0.5, 0.046875, ((0, 8), (1, 4)))
    gate_scale = jnp.clip(jnp.exp(math.log(4.0) - 2.7725887 * jax.random.uniform(seeds[2], (D // BLK, FFW // BLK), jnp.float32) ** block_scale(seeds[2], (D // BLK, FFW // BLK), ((0, 8), (1, 4)), -0.2, 0.2)), 0.25, 4.0)
    up_quant = normal_values(seeds[3], (D, FFW), D ** -0.5, 0.046875, ((0, 8), (1, 4)))
    up_scale = jnp.clip(jnp.exp(math.log(4.0) - 2.7725887 * jax.random.uniform(seeds[4], (D // BLK, FFW // BLK), jnp.float32) ** block_scale(seeds[4], (D // BLK, FFW // BLK), ((0, 8), (1, 4)), -0.2, 0.2)), 0.25, 4.0)
    down_quant = normal_values(seeds[5], (FFW, D), FFW ** -0.5, 0.0390625, ((0, 4), (1, 8)))
    down_scale = jnp.clip(jnp.exp(math.log(4.0) - 2.7725887 * jax.random.uniform(seeds[6], (FFW // BLK, D // BLK), jnp.float32) ** block_scale(seeds[6], (FFW // BLK, D // BLK), ((0, 4), (1, 8)), -0.2, 0.2)), 0.25, 4.0)
    return dict(tokens=tokens, gate_quant=gate_quant, gate_scale=gate_scale, up_quant=up_quant, up_scale=up_scale, down_quant=down_quant, down_scale=down_scale)


def dequant(quant, scale):
    rows, cols = quant.shape
    blocks = quant.astype(jnp.float32).reshape(rows // BLK, BLK, cols // BLK, BLK)
    return (blocks * scale[:, None, :, None]).reshape(rows, cols).astype(jnp.bfloat16)


def reference(tokens, gate_quant, gate_scale, up_quant, up_scale, down_quant, down_scale):
    width = D // N_WID

    def add_block(index, sums):
        gate_sum, up_sum = sums
        start = (index * width).astype(jnp.int32)
        rows_in = lax.dynamic_slice_in_dim(tokens, start, width, 1)
        gate_w = dequant(lax.dynamic_slice_in_dim(gate_quant, start, width, 0), lax.dynamic_slice_in_dim(gate_scale, start // BLK, width // BLK, 0))
        up_w = dequant(lax.dynamic_slice_in_dim(up_quant, start, width, 0), lax.dynamic_slice_in_dim(up_scale, start // BLK, width // BLK, 0))
        gate_part = jnp.dot(rows_in, gate_w, preferred_element_type=jnp.float32).astype(jnp.bfloat16)
        up_part = jnp.dot(rows_in, up_w, preferred_element_type=jnp.float32).astype(jnp.bfloat16)
        return (gate_sum + gate_part.astype(jnp.float32), up_sum + up_part.astype(jnp.float32))

    empty = jnp.zeros((ROWS, FFW), jnp.float32)
    gate, up = lax.fori_loop(0, N_WID, add_block, (empty, empty))
    hidden = (jax.nn.silu(gate) * up).astype(jnp.bfloat16)
    down_w = dequant(down_quant, down_scale)
    return jnp.dot(hidden, down_w, preferred_element_type=jnp.float32).astype(jnp.bfloat16)
```

```python
import functools

import jax
import jax.numpy as jnp
from jax import lax
from jax.experimental import pallas as pl
from jax.experimental.pallas import tpu as pltpu
from jax.sharding import PartitionSpec as P

BLK = 128
UNITS = 4 * BLK
GROUPS = 2
LAG_SUM = 1
LAG_HID = 1
MESH = pl.DeviceIdType.MESH


def kernel(
    n_hid, n_wid,
    x_ref, gq_ref, gs_ref, uq_ref, us_ref, dq_ref, ds_ref,
    out_ref,
    part, swap_out, swap_in, chain_in, hid, acc, gbuf, ubuf, dbuf, gu_w, down_w,
    share_out, share_in,
    w_sem, swap_s, swap_r, sum_s, sum_r, hid_s, hid_r, pair_s, pair_r,
    rs_s, rs_r, ag_s, ag_r,
):
    rows, depth = x_ref.shape
    width = out_ref.shape[1]
    chunks = gq_ref.shape[1] // UNITS
    rg = rows // GROUPS
    items = GROUPS * chunks
    chips = n_wid // 2
    slots = swap_out.shape[0]
    own_rows = rg // n_hid

    me_h, me_w = lax.axis_index("hid"), lax.axis_index("wid")
    core, chip = lax.rem(me_w, 2), lax.div(me_w, 2)
    sibling = (me_h, me_w + 1 - 2 * core)
    place = (chips - 1 - chip, chip)
    onward = ((me_h, me_w - 2), (me_h, me_w + 2))
    back = (onward[1], onward[0])

    def hid_peer(k):
        return (lax.rem(me_h + k, n_hid), me_w)

    barrier = pltpu.get_barrier_semaphore()

    def greet(dev):
        pl.semaphore_signal(barrier, inc=1, device_id=dev, device_id_type=MESH)

    greet(sibling)
    for k in range(1, n_hid):
        greet(hid_peer(k))

    @pl.when(chip > 0)
    def _():
        greet(onward[0])

    @pl.when(chip < chips - 1)
    def _():
        greet(onward[1])

    def gu_copies(j):
        cols = pl.ds(pl.multiple_of(j * UNITS, UNITS), UNITS)
        return (
            pltpu.make_async_copy(gq_ref.at[:, cols], gbuf, w_sem.at[0]),
            pltpu.make_async_copy(uq_ref.at[:, cols], ubuf, w_sem.at[1]),
        )

    def d_copy(j):
        units = pl.ds(pl.multiple_of(j * UNITS, UNITS), UNITS)
        return pltpu.make_async_copy(dq_ref.at[units], dbuf, w_sem.at[2])

    def remote(src, dst, send, recv, dev):
        return pltpu.make_async_remote_copy(
            src_ref=src, dst_ref=dst, send_sem=send, recv_sem=recv,
            device_id=dev, device_id_type=MESH,
        )

    def swap_copy(side, j):
        return remote(
            swap_out.at[lax.rem(j, slots), side], swap_in.at[side, j],
            swap_s.at[side, j], swap_r.at[side, j], sibling,
        )

    def split(i):
        g, j = lax.div(i, chunks), lax.rem(i, chunks)
        return j, pl.ds(pl.multiple_of(g * rg, rg), rg)

    def sum_copy(side, i):
        j, rs = split(i)
        return remote(
            part.at[side, j, rs], chain_in.at[side, j, rs],
            sum_s.at[side, i], sum_r.at[side, i], onward[side],
        )

    def hid_copy(side, i):
        j, rs = split(i)
        block = hid.at[j, 2 * side + core, rs]
        return remote(block, block, hid_s.at[side, i], hid_r.at[side, i], back[side])

    def pair_copy(side, i, whose):
        j, rs = split(i)
        block = hid.at[j, 2 * side + whose, rs]
        return remote(block, block, pair_s.at[side, i], pair_r.at[side, i], sibling)

    def rs_copy(g, k):
        to = lax.rem(me_h + k, n_hid)
        src = pl.ds(pl.multiple_of(g * rg + to * own_rows, own_rows), own_rows)
        return remote(
            share_out.at[src], share_in.at[g, k], rs_s.at[g, k], rs_r.at[g, k], hid_peer(k)
        )

    def ag_copy(g, k, owner):
        block = out_ref.at[pl.ds(pl.multiple_of(g * rg + owner * own_rows, own_rows), own_rows)]
        return remote(block, block, ag_s.at[g, k], ag_r.at[g, k], hid_peer(k))

    def project(j):
        for c in gu_copies(j):
            c.wait()

        def scale_rows(k, _):
            rs = pl.ds(pl.multiple_of(k * BLK, BLK), BLK)
            for qt in range(4):
                cs = slice(qt * BLK, (qt + 1) * BLK)
                for m, (buf, sc) in enumerate(((gbuf, gs_ref), (ubuf, us_ref))):
                    w = buf[rs, cs].astype(jnp.float32) * sc[k, j * 4 + qt]
                    gu_w[qt, rs, m * BLK : (m + 1) * BLK] = w.astype(jnp.bfloat16)
            return 0

        lax.fori_loop(0, depth // BLK, scale_rows, 0)

        @pl.when(j + 1 < chunks)
        def _():
            for c in gu_copies(j + 1):
                c.start()

        @pl.when(j >= slots)
        def _():
            for side in range(2):
                swap_copy(side, j - slots).wait_send()

        for side in range(2):
            theirs = jnp.dot(
                x_ref[...], gu_w[2 * side + 1 - core], preferred_element_type=jnp.float32
            )
            swap_out[lax.rem(j, slots), side] = theirs.astype(jnp.bfloat16)
            swap_copy(side, j).start()
        for side in range(2):
            mine = jnp.dot(
                x_ref[...], gu_w[2 * side + core], preferred_element_type=jnp.float32
            )
            part[side, j] = mine.astype(jnp.bfloat16)

    def sum_step(side, i):
        j, rs = split(i)

        @pl.when(i < chunks)
        def _():
            swap_copy(side, j).wait_recv()

        def own():
            return part[side, j, rs].astype(jnp.float32) + swap_in[side, j, rs].astype(jnp.float32)

        @pl.when(place[side] > 0)
        def _():
            sum_copy(side, i).wait_recv()

        @pl.when(place[side] == 0)
        def _():
            part[side, j, rs] = own().astype(jnp.bfloat16)

        @pl.when((place[side] > 0) & (place[side] < chips - 1))
        def _():
            s = own() + chain_in[side, j, rs].astype(jnp.float32)
            part[side, j, rs] = s.astype(jnp.bfloat16)

        @pl.when(place[side] < chips - 1)
        def _():
            sum_copy(side, i).start()

        @pl.when(place[side] == chips - 1)
        def _():
            s = own() + chain_in[side, j, rs].astype(jnp.float32)
            gate, up = s[:, :BLK], s[:, BLK:]
            h = gate / (1.0 + jnp.exp(-gate)) * up
            hid[j, 2 * side + core, rs] = h.astype(jnp.bfloat16)
            hid_copy(side, i).start()
            pair_copy(side, i, core).start()

    def hid_step(side, i):
        hid_copy(side, i).wait_recv()

        @pl.when(place[side] > 0)
        def _():
            hid_copy(side, i).start()

        pair_copy(side, i, core).start()

    def down_step(i):
        j, rs = split(i)
        d_copy(j).wait()

        def scale_rows(k, _):
            ks = pl.ds(pl.multiple_of(k * BLK, BLK), BLK)
            for b in range(width // BLK):
                cs = slice(b * BLK, (b + 1) * BLK)
                w = dbuf[ks, cs].astype(jnp.float32) * ds_ref[j * 4 + k, b]
                down_w[ks, cs] = w.astype(jnp.bfloat16)
            return 0

        lax.fori_loop(0, UNITS // BLK, scale_rows, 0)

        @pl.when(i + 1 < items)
        def _():
            d_copy(lax.rem(i + 1, chunks)).start()

        for side in range(2):
            pair_copy(side, i, 1 - core).wait_recv()
        h = jnp.concatenate([hid[j, qt, rs] for qt in range(4)], axis=1)
        for b in range(width // UNITS):
            cs = slice(b * UNITS, (b + 1) * UNITS)
            acc[rs, cs] += jnp.dot(h, down_w[:, cs], preferred_element_type=jnp.float32)

    def share_send(g):
        rs = slice(g * rg, (g + 1) * rg)
        share_out[rs] = acc[rs].astype(jnp.bfloat16)
        for k in range(1, n_hid):
            rs_copy(g, k).start()

    def share_sum(g):
        block = pl.ds(pl.multiple_of(g * rg + me_h * own_rows, own_rows), own_rows)
        total = share_out[block].astype(jnp.float32)
        for k in range(1, n_hid):
            rs_copy(g, k).wait_recv()
            total = total + share_in[g, k].astype(jnp.float32)
        out_ref[block] = total.astype(jnp.bfloat16)
        for k in range(1, n_hid):
            ag_copy(g, k, me_h).start()

    for c in gu_copies(0):
        c.start()
    d_copy(0).start()
    acc[...] = jnp.zeros_like(acc)
    pl.semaphore_wait(
        barrier,
        n_hid + jnp.where(chip > 0, 1, 0) + jnp.where(chip < chips - 1, 1, 0),
    )

    lag_hid0 = LAG_SUM * (chips - 1)
    lag_down = lag_hid0 + LAG_HID * (chips - 1) + 1
    steps = items + lag_down

    def step(t, _):
        for side in range(2):
            i = t - LAG_SUM * place[side]

            @pl.when((i >= 0) & (i < items))
            def _(side=side, i=i):
                sum_step(side, i)

        for side in range(2):
            hops = chips - 1 - place[side]
            i = t - lag_hid0 - LAG_HID * hops

            @pl.when((hops > 0) & (i >= 0) & (i < items))
            def _(side=side, i=i):
                hid_step(side, i)

        @pl.when(t + 1 < chunks)
        def _():
            project(t + 1)

        i = t - lag_down

        @pl.when(i >= 0)
        def _():
            down_step(i)

        for g in range(GROUPS - 1):
            done = lag_down + (g + 1) * chunks - 1

            @pl.when(t == done)
            def _(g=g):
                share_send(g)

            @pl.when(t == done + min(6, chunks - 1))
            def _(g=g):
                share_sum(g)

        return 0

    lax.fori_loop(-1, steps, step, 0)
    last = GROUPS - 1
    share_send(last)
    share_sum(last)

    for g in range(GROUPS):
        for k in range(1, n_hid):
            ag_copy(g, k, lax.rem(me_h + n_hid - k, n_hid)).wait_recv()
            rs_copy(g, k).wait_send()
            ag_copy(g, k, me_h).wait_send()

    def drain_swap(j, _):
        for side in range(2):
            swap_copy(side, j).wait_send()
        return 0

    lax.fori_loop(max(chunks - slots, 0), chunks, drain_swap, 0)

    def drain(i, _):
        for side in range(2):
            pair_copy(side, i, core).wait_send()

            @pl.when(place[side] < chips - 1)
            def _(side=side):
                sum_copy(side, i).wait_send()

            @pl.when(place[side] > 0)
            def _(side=side):
                hid_copy(side, i).wait_send()

        return 0

    lax.fori_loop(0, items, drain, 0)


def shards(n_hid, n_wid, tokens, gq, gs, uq, us, dq, ds):
    rows, depth = tokens.shape
    units, width = dq.shape
    chunks = units // UNITS
    items = GROUPS * chunks
    rg = rows // GROUPS
    bf16, f32 = jnp.bfloat16, jnp.float32
    dma = pltpu.SemaphoreType.DMA
    whole = pl.BlockSpec(memory_space=pltpu.VMEM)
    hbm = pl.BlockSpec(memory_space=pl.ANY)
    smem = pl.BlockSpec(memory_space=pltpu.SMEM)
    return pl.pallas_call(
        functools.partial(kernel, n_hid, n_wid),
        out_shape=jax.ShapeDtypeStruct((rows, width), bf16),
        in_specs=[whole, hbm, smem, hbm, smem, hbm, smem],
        out_specs=whole,
        scratch_shapes=[
            pltpu.VMEM((2, chunks, rows, 2 * BLK), bf16),
            pltpu.VMEM((2, 2, rows, 2 * BLK), bf16),
            pltpu.VMEM((2, chunks, rows, 2 * BLK), bf16),
            pltpu.VMEM((2, chunks, rows, 2 * BLK), bf16),
            pltpu.VMEM((chunks, 4, rows, BLK), bf16),
            pltpu.VMEM((rows, width), f32),
            pltpu.VMEM((depth, UNITS), bf16),
            pltpu.VMEM((depth, UNITS), bf16),
            pltpu.VMEM((UNITS, width), bf16),
            pltpu.VMEM((4, depth, 2 * BLK), bf16),
            pltpu.VMEM((UNITS, width), bf16),
            pltpu.VMEM((rows, width), bf16),
            pltpu.VMEM((GROUPS, n_hid, rg // n_hid, width), bf16),
            dma((3,)),
            dma((2, chunks)), dma((2, chunks)),
            dma((2, items)), dma((2, items)),
            dma((2, items)), dma((2, items)),
            dma((2, items)), dma((2, items)),
            dma((GROUPS, n_hid)), dma((GROUPS, n_hid)),
            dma((GROUPS, n_hid)), dma((GROUPS, n_hid)),
        ],
        compiler_params=pltpu.CompilerParams(
            collective_id=0, has_side_effects=True, vmem_limit_bytes=60 * 2**20
        ),
        cost_estimate=pl.CostEstimate(
            flops=6 * rows * depth * units,
            bytes_accessed=6 * depth * units,
            transcendentals=rows * units,
        ),
    )(tokens, gq, gs, uq, us, dq, ds)


def solution(mesh):
    return jax.shard_map(
        functools.partial(shards, mesh.shape["hid"], mesh.shape["wid"]),
        mesh=mesh,
        in_specs=(
            P(None, "wid"),
            P("wid", "hid"),
            P("wid", "hid"),
            P("wid", "hid"),
            P("wid", "hid"),
            P("hid", "wid"),
            P("hid", "wid"),
        ),
        out_specs=P(None, "wid"),
        check_vma=False,
    )
```

```python
import functools

import jax
import jax.numpy as jnp
from jax import lax
from jax.experimental import pallas as pl
from jax.experimental.pallas import tpu as pltpu
from jax.sharding import PartitionSpec as P

BLK = 128
UNITS = 4 * BLK
SUB = 128
LAG_SUM = 2
LAG_HID = 2
MESH = pl.DeviceIdType.MESH


def kernel(
    n_hid, n_wid,
    x_ref, gq_ref, gs_ref, uq_ref, us_ref, dq_ref, ds_ref,
    out_ref,
    part, swap_out, swap_in, chain_in, hid, acc, gbuf, ubuf, dbuf, gu_w, down_w,
    share_out, share_in0, share_in1,
    w_sem, swap_s, swap_r, sum_s, sum_r, hid_s, hid_r, pair_s, pair_r,
    rs_s, rs_r, ag_s, ag_r,
):
    rows, depth = x_ref.shape
    width = out_ref.shape[1]
    chunks = gq_ref.shape[1] // UNITS
    subs = rows // SUB - 1
    first = subs * chunks
    items = first + chunks
    chips = n_wid // 2
    slots = swap_out.shape[0]
    groups = ((0, subs * SUB, share_in0), (subs * SUB, SUB, share_in1))

    me_h, me_w = lax.axis_index("hid"), lax.axis_index("wid")
    core, chip = lax.rem(me_w, 2), lax.div(me_w, 2)
    sibling = (me_h, me_w + 1 - 2 * core)
    place = (chips - 1 - chip, chip)
    onward = ((me_h, me_w - 2), (me_h, me_w + 2))
    back = (onward[1], onward[0])

    def hid_peer(k):
        return (lax.rem(me_h + k, n_hid), me_w)

    barrier = pltpu.get_barrier_semaphore()

    def greet(dev):
        pl.semaphore_signal(barrier, inc=1, device_id=dev, device_id_type=MESH)

    greet(sibling)
    for k in range(1, n_hid):
        greet(hid_peer(k))

    @pl.when(chip > 0)
    def _():
        greet(onward[0])

    @pl.when(chip < chips - 1)
    def _():
        greet(onward[1])

    def gu_copies(j):
        cols = pl.ds(pl.multiple_of(j * UNITS, UNITS), UNITS)
        return (
            pltpu.make_async_copy(gq_ref.at[:, cols], gbuf, w_sem.at[0]),
            pltpu.make_async_copy(uq_ref.at[:, cols], ubuf, w_sem.at[1]),
        )

    def d_copy(j):
        units = pl.ds(pl.multiple_of(j * UNITS, UNITS), UNITS)
        return pltpu.make_async_copy(dq_ref.at[units], dbuf, w_sem.at[2])

    def remote(src, dst, send, recv, dev):
        return pltpu.make_async_remote_copy(
            src_ref=src, dst_ref=dst, send_sem=send, recv_sem=recv,
            device_id=dev, device_id_type=MESH,
        )

    def swap_copy(side, j):
        return remote(
            swap_out.at[lax.rem(j, slots), side], swap_in.at[side, j],
            swap_s.at[side, j], swap_r.at[side, j], sibling,
        )

    def split(i):
        late = i >= first
        j = jnp.where(late, i - first, lax.div(i, subs))
        r = jnp.where(late, subs, lax.rem(i, subs))
        return j, pl.ds(pl.multiple_of(r * SUB, SUB), SUB)

    def sum_copy(side, i):
        j, rs = split(i)
        return remote(
            part.at[side, j, rs], chain_in.at[side, j, rs],
            sum_s.at[side, i], sum_r.at[side, i], onward[side],
        )

    def hid_copy(side, i):
        j, rs = split(i)
        block = hid.at[j, 2 * side + core, rs]
        return remote(block, block, hid_s.at[side, i], hid_r.at[side, i], back[side])

    def pair_copy(side, i, whose):
        j, rs = split(i)
        block = hid.at[j, 2 * side + whose, rs]
        return remote(block, block, pair_s.at[side, i], pair_r.at[side, i], sibling)

    def owned(g, owner):
        start, size, _ = groups[g]
        n = size // n_hid
        return pl.ds(pl.multiple_of(start + owner * n, n), n)

    def rs_copy(g, k):
        src = share_out.at[owned(g, lax.rem(me_h + k, n_hid))]
        return remote(src, groups[g][2].at[k], rs_s.at[g, k], rs_r.at[g, k], hid_peer(k))

    def ag_copy(g, k, owner):
        block = out_ref.at[owned(g, owner)]
        return remote(block, block, ag_s.at[g, k], ag_r.at[g, k], hid_peer(k))

    def spread(scale):
        return jnp.full((BLK, BLK), scale, jnp.float32).astype(jnp.bfloat16)

    def scale_gu(j):
        for c in gu_copies(j):
            c.wait()

        def scale_rows(k, _):
            rs = pl.ds(pl.multiple_of(k * BLK, BLK), BLK)
            for qt in range(4):
                cs = slice(qt * BLK, (qt + 1) * BLK)
                for m, (buf, sc) in enumerate(((gbuf, gs_ref), (ubuf, us_ref))):
                    gu_w[qt, rs, m * BLK : (m + 1) * BLK] = buf[rs, cs] * spread(sc[k, j * 4 + qt])
            return 0

        lax.fori_loop(0, depth // BLK, scale_rows, 0)

        @pl.when(j + 1 < chunks)
        def _():
            for c in gu_copies(j + 1):
                c.start()

    def project_theirs(side, j):
        @pl.when(j >= slots)
        def _():
            swap_copy(side, j - slots).wait_send()

        theirs = jnp.dot(
            x_ref[...], gu_w[2 * side + 1 - core], preferred_element_type=jnp.float32
        )
        swap_out[lax.rem(j, slots), side] = theirs.astype(jnp.bfloat16)
        swap_copy(side, j).start()

    def project_mine(side, j):
        mine = jnp.dot(
            x_ref[...], gu_w[2 * side + core], preferred_element_type=jnp.float32
        )
        part[side, j] = mine.astype(jnp.bfloat16)

    def sum_step(side, i):
        j, rs = split(i)

        @pl.when((i < first) & (lax.rem(i, subs) == 0))
        def _():
            swap_copy(side, j).wait_recv()

        def own():
            return part[side, j, rs].astype(jnp.float32) + swap_in[side, j, rs].astype(jnp.float32)

        @pl.when(place[side] > 0)
        def _():
            sum_copy(side, i).wait_recv()

        @pl.when(place[side] == 0)
        def _():
            part[side, j, rs] = own().astype(jnp.bfloat16)

        @pl.when((place[side] > 0) & (place[side] < chips - 1))
        def _():
            s = own() + chain_in[side, j, rs].astype(jnp.float32)
            part[side, j, rs] = s.astype(jnp.bfloat16)

        @pl.when(place[side] < chips - 1)
        def _():
            sum_copy(side, i).start()

        @pl.when(place[side] == chips - 1)
        def _():
            s = own() + chain_in[side, j, rs].astype(jnp.float32)
            gate, up = s[:, :BLK], s[:, BLK:]
            h = gate / (1.0 + jnp.exp(-gate)) * up
            hid[j, 2 * side + core, rs] = h.astype(jnp.bfloat16)
            hid_copy(side, i).start()
            pair_copy(side, i, core).start()

    def hid_step(side, i):
        hid_copy(side, i).wait_recv()

        @pl.when(place[side] > 0)
        def _():
            hid_copy(side, i).start()

        pair_copy(side, i, core).start()

    def scale_down(j, more):
        d_copy(j).wait()

        def scale_rows(k, _):
            ks = pl.ds(pl.multiple_of(k * BLK, BLK), BLK)
            for b in range(width // BLK):
                cs = slice(b * BLK, (b + 1) * BLK)
                down_w[ks, cs] = dbuf[ks, cs] * spread(ds_ref[j * 4 + k, b])
            return 0

        lax.fori_loop(0, UNITS // BLK, scale_rows, 0)

        @pl.when(more)
        def _():
            d_copy(lax.rem(j + 1, chunks)).start()

    def down_step(i):
        j, rs = split(i)

        @pl.when((i >= first) | (lax.rem(i, subs) == 0))
        def _():
            scale_down(j, i + 1 < items)

        for side in range(2):
            pair_copy(side, i, 1 - core).wait_recv()
        h = jnp.concatenate([hid[j, qt, rs] for qt in range(4)], axis=1)
        for b in range(width // UNITS):
            cs = slice(b * UNITS, (b + 1) * UNITS)
            acc[rs, cs] += jnp.dot(h, down_w[:, cs], preferred_element_type=jnp.float32)

    def share_send(g):
        start, size, _ = groups[g]
        rs = slice(start, start + size)
        share_out[rs] = acc[rs].astype(jnp.bfloat16)
        for k in range(1, n_hid):
            rs_copy(g, k).start()

    def share_sum(g):
        block = owned(g, me_h)
        total = share_out[block].astype(jnp.float32)
        for k in range(1, n_hid):
            rs_copy(g, k).wait_recv()
            total = total + groups[g][2][k].astype(jnp.float32)
        out_ref[block] = total.astype(jnp.bfloat16)
        for k in range(1, n_hid):
            ag_copy(g, k, me_h).start()

    for c in gu_copies(0):
        c.start()
    d_copy(0).start()
    acc[...] = jnp.zeros_like(acc)
    pl.semaphore_wait(
        barrier,
        n_hid + jnp.where(chip > 0, 1, 0) + jnp.where(chip < chips - 1, 1, 0),
    )

    scale_gu(0)
    for side in range(2):
        project_theirs(side, 0)
    for side in range(2):
        project_mine(side, 0)

    lag_hid0 = LAG_SUM * (chips - 1)
    lag_down = lag_hid0 + LAG_HID * (chips - 1) + 1
    steps = items + lag_down

    def step(t, _):
        for side in range(2):
            i = t - LAG_SUM * place[side]

            @pl.when((i >= 0) & (i < items))
            def _(side=side, i=i):
                sum_step(side, i)

        for side in range(2):
            hops = chips - 1 - place[side]
            i = t - lag_hid0 - LAG_HID * hops

            @pl.when((hops > 0) & (i >= 0) & (i < items))
            def _(side=side, i=i):
                hid_step(side, i)

        j, phase = lax.div(t, subs) + 1, lax.rem(t, subs)

        @pl.when((j < chunks) & (phase == 0))
        def _():
            scale_gu(j)
            project_theirs(0, j)

        @pl.when((j < chunks) & (phase == min(1, subs - 1)))
        def _():
            project_theirs(1, j)

        @pl.when((j < chunks) & (phase == subs - 1))
        def _():
            project_mine(0, j)
            project_mine(1, j)

        i = t - lag_down

        @pl.when(i >= 0)
        def _():
            down_step(i)

        done = lag_down + first - 1

        @pl.when(t == done)
        def _():
            share_send(0)

        @pl.when(t == done + min(9, chunks - 1))
        def _():
            share_sum(0)

        return 0

    lax.fori_loop(0, steps, step, 0)
    share_send(1)
    share_sum(1)

    for g in range(2):
        for k in range(1, n_hid):
            ag_copy(g, k, lax.rem(me_h + n_hid - k, n_hid)).wait_recv()
            rs_copy(g, k).wait_send()
            ag_copy(g, k, me_h).wait_send()

    def drain_swap(j, _):
        for side in range(2):
            swap_copy(side, j).wait_send()
        return 0

    lax.fori_loop(max(chunks - slots, 0), chunks, drain_swap, 0)

    def drain(i, _):
        for side in range(2):
            pair_copy(side, i, core).wait_send()

            @pl.when(place[side] < chips - 1)
            def _(side=side):
                sum_copy(side, i).wait_send()

            @pl.when(place[side] > 0)
            def _(side=side):
                hid_copy(side, i).wait_send()

        return 0

    lax.fori_loop(0, items, drain, 0)


def shards(n_hid, n_wid, tokens, gq, gs, uq, us, dq, ds):
    rows, depth = tokens.shape
    units, width = dq.shape
    chunks = units // UNITS
    items = rows // SUB * chunks
    bf16, f32 = jnp.bfloat16, jnp.float32
    dma = pltpu.SemaphoreType.DMA
    whole = pl.BlockSpec(memory_space=pltpu.VMEM)
    hbm = pl.BlockSpec(memory_space=pl.ANY)
    smem = pl.BlockSpec(memory_space=pltpu.SMEM)
    return pl.pallas_call(
        functools.partial(kernel, n_hid, n_wid),
        out_shape=jax.ShapeDtypeStruct((rows, width), bf16),
        in_specs=[whole, hbm, smem, hbm, smem, hbm, smem],
        out_specs=whole,
        scratch_shapes=[
            pltpu.VMEM((2, chunks, rows, 2 * BLK), bf16),
            pltpu.VMEM((2, 2, rows, 2 * BLK), bf16),
            pltpu.VMEM((2, chunks, rows, 2 * BLK), bf16),
            pltpu.VMEM((2, chunks, rows, 2 * BLK), bf16),
            pltpu.VMEM((chunks, 4, rows, BLK), bf16),
            pltpu.VMEM((rows, width), f32),
            pltpu.VMEM((depth, UNITS), bf16),
            pltpu.VMEM((depth, UNITS), bf16),
            pltpu.VMEM((UNITS, width), bf16),
            pltpu.VMEM((4, depth, 2 * BLK), bf16),
            pltpu.VMEM((UNITS, width), bf16),
            pltpu.VMEM((rows, width), bf16),
            pltpu.VMEM((n_hid, (rows - SUB) // n_hid, width), bf16),
            pltpu.VMEM((n_hid, SUB // n_hid, width), bf16),
            dma((3,)),
            dma((2, chunks)), dma((2, chunks)),
            dma((2, items)), dma((2, items)),
            dma((2, items)), dma((2, items)),
            dma((2, items)), dma((2, items)),
            dma((2, n_hid)), dma((2, n_hid)),
            dma((2, n_hid)), dma((2, n_hid)),
        ],
        compiler_params=pltpu.CompilerParams(
            collective_id=0, has_side_effects=True, vmem_limit_bytes=60 * 2**20
        ),
        cost_estimate=pl.CostEstimate(
            flops=6 * rows * depth * units,
            bytes_accessed=6 * depth * units,
            transcendentals=rows * units,
        ),
    )(tokens, gq, gs, uq, us, dq, ds)


def solution(mesh):
    return jax.shard_map(
        functools.partial(shards, mesh.shape["hid"], mesh.shape["wid"]),
        mesh=mesh,
        in_specs=(
            P(None, "wid"),
            P("wid", "hid"),
            P("wid", "hid"),
            P("wid", "hid"),
            P("wid", "hid"),
            P("hid", "wid"),
            P("hid", "wid"),
        ),
        out_specs=P(None, "wid"),
        check_vma=False,
    )
```

```python
import functools

import jax
import jax.numpy as jnp
from jax import lax
from jax.experimental import pallas as pl
from jax.experimental.pallas import tpu as pltpu
from jax.sharding import PartitionSpec as P

BLK = 128
UNITS = 4 * BLK
SUB = 128
LAG_SUM = 2
LAG_HID = 2
MESH = pl.DeviceIdType.MESH


def kernel(
    n_hid, n_wid,
    x_ref, gq_ref, gs_ref, uq_ref, us_ref, dq_ref, ds_ref,
    out_ref,
    part, swap_out, swap_in, chain_in, hid, acc, gbuf, ubuf, dbuf,
    share_out, share_in0, share_in1,
    w_sem, swap_s, swap_r, sum_s, sum_r, hid_s, hid_r, pair_s, pair_r,
    rs_s, rs_r, ag_s, ag_r,
):
    rows, depth = x_ref.shape
    width = out_ref.shape[1]
    chunks = gq_ref.shape[1] // UNITS
    subs = rows // SUB - 1
    first = subs * chunks
    items = first + chunks
    chips = n_wid // 2
    slots = swap_out.shape[0]
    groups = ((0, subs * SUB, share_in0), (subs * SUB, SUB, share_in1))

    me_h, me_w = lax.axis_index("hid"), lax.axis_index("wid")
    core, chip = lax.rem(me_w, 2), lax.div(me_w, 2)
    sibling = (me_h, me_w + 1 - 2 * core)
    place = (chips - 1 - chip, chip)
    onward = ((me_h, me_w - 2), (me_h, me_w + 2))
    back = (onward[1], onward[0])

    def hid_peer(k):
        return (lax.rem(me_h + k, n_hid), me_w)

    barrier = pltpu.get_barrier_semaphore()

    def greet(dev):
        pl.semaphore_signal(barrier, inc=1, device_id=dev, device_id_type=MESH)

    greet(sibling)
    for k in range(1, n_hid):
        greet(hid_peer(k))

    @pl.when(chip > 0)
    def _():
        greet(onward[0])

    @pl.when(chip < chips - 1)
    def _():
        greet(onward[1])

    def gu_copies(j):
        cols = pl.ds(pl.multiple_of(j * UNITS, UNITS), UNITS)
        slot = lax.rem(j, 2)
        return (
            pltpu.make_async_copy(gq_ref.at[:, cols], gbuf.at[slot], w_sem.at[0, slot]),
            pltpu.make_async_copy(uq_ref.at[:, cols], ubuf.at[slot], w_sem.at[1, slot]),
        )

    def d_copy(n):
        units = pl.ds(pl.multiple_of(lax.rem(n, chunks) * UNITS, UNITS), UNITS)
        slot = lax.rem(n, 2)
        return pltpu.make_async_copy(dq_ref.at[units], dbuf.at[slot], w_sem.at[2, slot])

    def remote(src, dst, send, recv, dev):
        return pltpu.make_async_remote_copy(
            src_ref=src, dst_ref=dst, send_sem=send, recv_sem=recv,
            device_id=dev, device_id_type=MESH,
        )

    def swap_copy(side, j):
        return remote(
            swap_out.at[lax.rem(j, slots), side], swap_in.at[side, j],
            swap_s.at[side, j], swap_r.at[side, j], sibling,
        )

    def split(i):
        late = i >= first
        j = jnp.where(late, i - first, lax.div(i, subs))
        r = jnp.where(late, subs, lax.rem(i, subs))
        return j, pl.ds(pl.multiple_of(r * SUB, SUB), SUB)

    def sum_copy(side, i):
        j, rs = split(i)
        return remote(
            part.at[side, j, rs], chain_in.at[side, j, rs],
            sum_s.at[side, i], sum_r.at[side, i], onward[side],
        )

    def hid_copy(side, i):
        j, rs = split(i)
        block = hid.at[j, 2 * side + core, rs]
        return remote(block, block, hid_s.at[side, i], hid_r.at[side, i], back[side])

    def pair_copy(side, i, whose):
        j, rs = split(i)
        block = hid.at[j, 2 * side + whose, rs]
        return remote(block, block, pair_s.at[side, i], pair_r.at[side, i], sibling)

    def owned(g, owner):
        start, size, _ = groups[g]
        n = size // n_hid
        return pl.ds(pl.multiple_of(start + owner * n, n), n)

    def rs_copy(g, k):
        src = share_out.at[owned(g, lax.rem(me_h + k, n_hid))]
        return remote(src, groups[g][2].at[k], rs_s.at[g, k], rs_r.at[g, k], hid_peer(k))

    def ag_copy(g, k, owner):
        block = out_ref.at[owned(g, owner)]
        return remote(block, block, ag_s.at[g, k], ag_r.at[g, k], hid_peer(k))

    def spread(scale):
        return jnp.full((BLK, BLK), scale, jnp.float32).astype(jnp.bfloat16)

    def load_gu(j):
        for c in gu_copies(j):
            c.wait()

        @pl.when(j + 1 < chunks)
        def _():
            for c in gu_copies(j + 1):
                c.start()

    def project(qt, j):
        slot = lax.rem(j, 2)
        cols = pl.ds(pl.multiple_of(qt * BLK, BLK), BLK)
        halves = []
        for buf, sc in ((gbuf, gs_ref), (ubuf, us_ref)):
            blocks = [
                buf[slot, k * BLK : (k + 1) * BLK, cols] * spread(sc[k, j * 4 + qt])
                for k in range(depth // BLK)
            ]
            halves.append(jnp.concatenate(blocks, axis=0))
        w = jnp.concatenate(halves, axis=1)
        both = jnp.dot(x_ref[...], w, preferred_element_type=jnp.float32)
        return both.astype(jnp.bfloat16)

    def project_theirs(side, j):
        @pl.when(j >= slots)
        def _():
            swap_copy(side, j - slots).wait_send()

        swap_out[lax.rem(j, slots), side] = project(2 * side + 1 - core, j)
        swap_copy(side, j).start()

    def project_mine(side, j):
        part[side, j] = project(2 * side + core, j)

    def sum_step(side, i):
        j, rs = split(i)

        @pl.when((i < first) & (lax.rem(i, subs) == 0))
        def _():
            swap_copy(side, j).wait_recv()

        def own():
            return part[side, j, rs].astype(jnp.float32) + swap_in[side, j, rs].astype(jnp.float32)

        @pl.when(place[side] > 0)
        def _():
            sum_copy(side, i).wait_recv()

        @pl.when(place[side] == 0)
        def _():
            part[side, j, rs] = own().astype(jnp.bfloat16)

        @pl.when((place[side] > 0) & (place[side] < chips - 1))
        def _():
            s = own() + chain_in[side, j, rs].astype(jnp.float32)
            part[side, j, rs] = s.astype(jnp.bfloat16)

        @pl.when(place[side] < chips - 1)
        def _():
            sum_copy(side, i).start()

        @pl.when(place[side] == chips - 1)
        def _():
            s = own() + chain_in[side, j, rs].astype(jnp.float32)
            gate, up = s[:, :BLK], s[:, BLK:]
            h = gate / (1.0 + jnp.exp(-gate)) * up
            hid[j, 2 * side + core, rs] = h.astype(jnp.bfloat16)
            hid_copy(side, i).start()
            pair_copy(side, i, core).start()

    def hid_step(side, i):
        hid_copy(side, i).wait_recv()

        @pl.when(place[side] > 0)
        def _():
            hid_copy(side, i).start()

        pair_copy(side, i, core).start()

    def down_step(i):
        j, rs = split(i)
        n = jnp.where(i >= first, chunks, 0) + j
        slot = lax.rem(n, 2)

        @pl.when((i >= first) | (lax.rem(i, subs) == 0))
        def _():
            d_copy(n).wait()

            @pl.when(n + 1 < 2 * chunks)
            def _():
                d_copy(n + 1).start()

        for side in range(2):
            pair_copy(side, i, 1 - core).wait_recv()
        h = jnp.concatenate([hid[j, qt, rs] for qt in range(4)], axis=1)
        for b in range(width // UNITS):
            cs = slice(b * UNITS, (b + 1) * UNITS)
            w = jnp.concatenate(
                [
                    jnp.concatenate(
                        [
                            dbuf[slot, k * BLK : (k + 1) * BLK, m * BLK : (m + 1) * BLK]
                            * spread(ds_ref[j * 4 + k, m])
                            for m in range(b * 4, b * 4 + 4)
                        ],
                        axis=1,
                    )
                    for k in range(4)
                ],
                axis=0,
            )
            acc[rs, cs] += jnp.dot(h, w, preferred_element_type=jnp.float32)

    def share_send(g):
        start, size, _ = groups[g]
        rs = slice(start, start + size)
        share_out[rs] = acc[rs].astype(jnp.bfloat16)
        for k in range(1, n_hid):
            rs_copy(g, k).start()

    def share_sum(g):
        block = owned(g, me_h)
        total = share_out[block].astype(jnp.float32)
        for k in range(1, n_hid):
            rs_copy(g, k).wait_recv()
            total = total + groups[g][2][k].astype(jnp.float32)
        out_ref[block] = total.astype(jnp.bfloat16)
        for k in range(1, n_hid):
            ag_copy(g, k, me_h).start()

    for c in gu_copies(0):
        c.start()
    d_copy(0).start()
    acc[...] = jnp.zeros_like(acc)
    pl.semaphore_wait(
        barrier,
        n_hid + jnp.where(chip > 0, 1, 0) + jnp.where(chip < chips - 1, 1, 0),
    )

    load_gu(0)
    for side in range(2):
        project_theirs(side, 0)
    for side in range(2):
        project_mine(side, 0)

    lag_hid0 = LAG_SUM * (chips - 1)
    lag_down = lag_hid0 + LAG_HID * (chips - 1) + 1
    steps = items + lag_down

    def step(t, _):
        for side in range(2):
            i = t - LAG_SUM * place[side]

            @pl.when((i >= 0) & (i < items))
            def _(side=side, i=i):
                sum_step(side, i)

        for side in range(2):
            hops = chips - 1 - place[side]
            i = t - lag_hid0 - LAG_HID * hops

            @pl.when((hops > 0) & (i >= 0) & (i < items))
            def _(side=side, i=i):
                hid_step(side, i)

        j, phase = lax.div(t, subs) + 1, lax.rem(t, subs)

        @pl.when((j < chunks) & (phase == 0))
        def _():
            load_gu(j)
            project_theirs(0, j)

        @pl.when((j < chunks) & (phase == min(1, subs - 1)))
        def _():
            project_theirs(1, j)

        @pl.when((j < chunks) & (phase == subs - 1))
        def _():
            project_mine(0, j)
            project_mine(1, j)

        i = t - lag_down

        @pl.when(i >= 0)
        def _():
            down_step(i)

        done = lag_down + first - 1

        @pl.when(t == done)
        def _():
            share_send(0)

        @pl.when(t == done + min(9, chunks - 1))
        def _():
            share_sum(0)

        return 0

    lax.fori_loop(0, steps, step, 0)
    share_send(1)
    share_sum(1)

    for g in range(2):
        for k in range(1, n_hid):
            ag_copy(g, k, lax.rem(me_h + n_hid - k, n_hid)).wait_recv()
            rs_copy(g, k).wait_send()
            ag_copy(g, k, me_h).wait_send()

    def drain_swap(j, _):
        for side in range(2):
            swap_copy(side, j).wait_send()
        return 0

    lax.fori_loop(max(chunks - slots, 0), chunks, drain_swap, 0)

    def drain(i, _):
        for side in range(2):
            pair_copy(side, i, core).wait_send()

            @pl.when(place[side] < chips - 1)
            def _(side=side):
                sum_copy(side, i).wait_send()

            @pl.when(place[side] > 0)
            def _(side=side):
                hid_copy(side, i).wait_send()

        return 0

    lax.fori_loop(0, items, drain, 0)


def shards(n_hid, n_wid, tokens, gq, gs, uq, us, dq, ds):
    rows, depth = tokens.shape
    units, width = dq.shape
    chunks = units // UNITS
    items = rows // SUB * chunks
    bf16, f32 = jnp.bfloat16, jnp.float32
    dma = pltpu.SemaphoreType.DMA
    whole = pl.BlockSpec(memory_space=pltpu.VMEM)
    hbm = pl.BlockSpec(memory_space=pl.ANY)
    smem = pl.BlockSpec(memory_space=pltpu.SMEM)
    return pl.pallas_call(
        functools.partial(kernel, n_hid, n_wid),
        out_shape=jax.ShapeDtypeStruct((rows, width), bf16),
        in_specs=[whole, hbm, smem, hbm, smem, hbm, smem],
        out_specs=whole,
        scratch_shapes=[
            pltpu.VMEM((2, chunks, rows, 2 * BLK), bf16),
            pltpu.VMEM((2, 2, rows, 2 * BLK), bf16),
            pltpu.VMEM((2, chunks, rows, 2 * BLK), bf16),
            pltpu.VMEM((2, chunks, rows, 2 * BLK), bf16),
            pltpu.VMEM((chunks, 4, rows, BLK), bf16),
            pltpu.VMEM((rows, width), f32),
            pltpu.VMEM((2, depth, UNITS), bf16),
            pltpu.VMEM((2, depth, UNITS), bf16),
            pltpu.VMEM((2, UNITS, width), bf16),
            pltpu.VMEM((rows, width), bf16),
            pltpu.VMEM((n_hid, (rows - SUB) // n_hid, width), bf16),
            pltpu.VMEM((n_hid, SUB // n_hid, width), bf16),
            dma((3, 2)),
            dma((2, chunks)), dma((2, chunks)),
            dma((2, items)), dma((2, items)),
            dma((2, items)), dma((2, items)),
            dma((2, items)), dma((2, items)),
            dma((2, n_hid)), dma((2, n_hid)),
            dma((2, n_hid)), dma((2, n_hid)),
        ],
        compiler_params=pltpu.CompilerParams(
            collective_id=0, has_side_effects=True, vmem_limit_bytes=60 * 2**20
        ),
        cost_estimate=pl.CostEstimate(
            flops=6 * rows * depth * units,
            bytes_accessed=6 * depth * units,
            transcendentals=rows * units,
        ),
    )(tokens, gq, gs, uq, us, dq, ds)


def solution(mesh):
    return jax.shard_map(
        functools.partial(shards, mesh.shape["hid"], mesh.shape["wid"]),
        mesh=mesh,
        in_specs=(
            P(None, "wid"),
            P("wid", "hid"),
            P("wid", "hid"),
            P("wid", "hid"),
            P("wid", "hid"),
            P("hid", "wid"),
            P("hid", "wid"),
        ),
        out_specs=P(None, "wid"),
        check_vma=False,
    )
```
